32 devices in a mesh: groups: 2 (over x), space: 16 (over z, y, core).
Axes of the slice: x: 2, y: 2, z: 4, core: 2. Of those that a mesh axis runs over, the one named last changes fastest.
Arguments:
- eigvecs: bfloat16 [2, 384, 3, 12288], P(None, None, None, ('groups', 'space')), parts along dimension 3, may hold values from -1.5 to 1.5
- momenta: int32 [4, 3], replicated, may hold values from -2 to 2
- peram: bfloat16 [32, 2, 384, 384], P(('groups', 'space')), parts along dimension 0, may hold values from -0.21875 to 0.21875
- graph: int32 [3072, 8], P(('groups', 'space')), parts along dimension 0, may hold values from 0 to 15, all different within a row; in each aligned block of 96 rows (0 to 95, 96 to 191, ...) at most 96 rows name the same one
Outputs:
- contracted: bfloat16 [3072, 8, 768], P(('groups', 'space')), parts along dimension 0
The draws below stay inside these ranges and needn't reach their ends.
There are 2 independent parts, one for each index of `groups`. The reference program is written for one: setup_inputs(seed, part) draws one part's arguments, and reference() takes and returns one part's arrays. A program takes and returns all parts, laid end to end along the dimension named above; an argument that names none is the same for every part. Nothing has to cross between parts.
Inputs may be any that keep to these rules, and one draw needn't show every extreme that they name: `graph`: each row names 8 different owners; among the rows of one device no owner is named more than 96 times, a bound that some block reaches.
All inputs are finite; a program needn't handle non-finite values.
Results may differ from the reference program's by a relative error of at most 0.0064.
Values may be sent and summed in bfloat16 or wider, within the bound.
No kernel may reach another device: no remote copies, remote signals or barrier semaphores. Data moves between devices by JAX's collectives and lax.ppermute only.
A program may use at most 64 MiB of HBM per device.

```python
import math
import jax
import jax.numpy as jnp
import numpy as np
from jax import lax

N = 384
MOMENTA = 4
EXTENT = 128
SITES = 6144
ROWS = 1536
ROWS_DEV = 96
OWNERS = 16
FANOUT = 8
CAP = 96


def plant(entries, key, least, high):
    place = [jax.random.randint(jax.random.fold_in(key, axis), (), 0, length) for axis, length in enumerate(entries.shape)]
    widest = entries.shape.index(max(entries.shape))
    beside = place[:widest] + [(place[widest] + 1) % entries.shape[widest]] + place[widest + 1:]
    return entries.at[tuple(place)].set(least).at[tuple(beside)].set(high)


def with_spikes(values, rng, source, target, shards_of, factor):
    def block_of(position):
        return (jnp.arange(values.shape[position]) // (values.shape[position] // shards_of)).reshape((-1,) + (1,) * (values.ndim - 1 - position))

    near = jax.random.permutation(rng, shards_of)[block_of(target)]
    far = (block_of(target) + shards_of // 2) % shards_of
    return jnp.where((block_of(source) == near) | (block_of(source) == far), factor * values, values)


def block_scale(stream_key, shape, shards, least, high):
    gain = 1.0
    for axis_at, shards_of in shards:
        heights = jax.random.uniform(jax.random.fold_in(jax.random.fold_in(stream_key, 6), axis_at), (shards_of,), jnp.float32, least / len(shards), high / len(shards))
        gain = gain * jnp.repeat(jnp.exp(heights), shape[axis_at] // shards_of).reshape((-1,) + (1,) * (len(shape) - 1 - axis_at))
    return gain


def assign_block(rng, own, number, rows, number_of, top, most, skew):
    sequence = jax.random.permutation(rng, number_of)
    packed, ordinary = load_shares(number_of, rows * top, most, skew, True), load_shares(number_of, rows * top, most, skew, False)
    places = jnp.arange(number_of)

    def named(tallies, turn):
        used = int((tallies > 0).sum())
        fixed = max(1, used // 4)
        moved = fixed + (places - fixed + turn * (used - fixed)) % max(1, number_of - fixed)
        return jnp.zeros((number_of,), jnp.int32).at[sequence[jnp.where(places < fixed, places, moved)]].set(jnp.asarray(tallies, jnp.int32))

    tallies = jnp.where(number % 4 == 0, named(packed, number // 4), named(ordinary, number - number // 4 - 1))
    mixed = jax.random.permutation(jax.random.fold_in(own, 3), number_of)
    donor, sink = mixed[0:number_of // 2 * 2:2], mixed[1:number_of // 2 * 2:2]
    slack = jnp.minimum(tallies[donor] - 1, most - tallies[sink]) // 2
    slack = jnp.where((donor == sequence[0]) | (sink == sequence[0]) | (tallies[sink] == 0), 0, jnp.maximum(slack, 0))
    moved = jax.random.randint(jax.random.fold_in(own, 4), (number_of // 2,), 0, 1 << 20) % (slack + 1)
    tallies = tallies.at[donor].add(-moved).at[sink].add(moved)
    labels = jnp.searchsorted(jnp.cumsum(tallies), jnp.arange(rows * top), side="right").astype(jnp.int32)
    table = labels.reshape(top, rows).T
    table = table[jax.random.permutation(jax.random.fold_in(own, 1), rows)]
    turn = jax.random.randint(jax.random.fold_in(own, 2), (rows, 1), 0, top)
    return jnp.take_along_axis(table, (jnp.arange(top)[None, :] + turn) % top, axis=1)


def load_shares(count, total, bound, slope, full):
    weights = [(1 << 20) // math.isqrt(rank ** slope) + 1 for rank in range(1, count + 1)]
    largest = bound if full else min(bound, max(-(-total // count), total * weights[0] // sum(weights)))
    least = 1 if total - largest >= count - 1 else 0
    counts, spare = [largest] + [least] * (count - 1), total - largest - least * (count - 1)
    while spare > 0:
        movable = [i for i in range(1, count) if counts[i] < largest] or [i for i in range(1, count) if counts[i] < bound]
        mass, budget = sum([weights[i] for i in movable]), spare
        for i in movable:
            more = min(bound - counts[i], max(1, budget * weights[i] // mass), spare)
            counts[i] = counts[i] + more
            spare = spare - more
    return np.array(counts)


def gaussian(stream_key, shape, width, reach, pieces=(), kind=jnp.bfloat16):
    gain = block_scale(stream_key, shape, pieces, -0.22, 0.18) if pieces else 1.0
    drawn = jax.random.normal(stream_key, shape, jnp.float32) * width * gain
    return jnp.minimum(jnp.maximum(drawn, -reach), reach).astype(kind)


def noise_with(own_key, dims, width, reach, split, heavy, held_as=jnp.bfloat16):
    values = width * jax.random.normal(own_key, dims, jnp.float32)
    if split:
        values = values * block_scale(own_key, dims, split, -0.22, 0.18)
    return jnp.clip(with_spikes(values, jax.random.fold_in(own_key, 3), *heavy), -reach, reach).astype(held_as)


def setup_inputs(seed: int = 0, part: int = 0) -> dict:
    splits = jax.random.split(jax.random.key(seed), 5)
    part_splits = jax.random.split(jax.random.fold_in(splits[4], part), 5)
    eigvecs = noise_with(part_splits[0], (2, N, 3, SITES), ((6 * SITES) ** -0.25), 1.5, ((3, 16),), (3, 1, 16, 2.0))
    momenta = plant(jax.random.randint(splits[1], (MOMENTA, 3), -2, 3), jax.random.fold_in(splits[1], 1), -2, 2).astype(jnp.int32)
    peram = gaussian(part_splits[2], (OWNERS, 2, N, N), (2 * N) ** -0.5, 0.21875, ((0, 16),))
    graph_keys = jax.random.split(jax.random.fold_in(part_splits[3], 1), ROWS // ROWS_DEV)
    graph_turns = jax.random.permutation(jax.random.fold_in(part_splits[3], 3), ROWS // ROWS_DEV)
    graph = jax.vmap(lambda own, number: assign_block(jax.random.fold_in(part_splits[3], 2), own, number, ROWS_DEV, OWNERS, FANOUT, CAP, 2))(graph_keys, graph_turns).reshape((ROWS, FANOUT))
    return dict(eigvecs=eigvecs, momenta=momenta, peram=peram, graph=graph)


def phase_tables(momenta, site_index, extent):
    coord_x = site_index % extent
    coord_y = (site_index // extent) % extent
    coord_z = site_index // (extent * extent)
    wave_number = momenta[:, 0:1] * coord_x[None, :] + momenta[:, 1:2] * coord_y[None, :] + momenta[:, 2:3] * coord_z[None, :]
    wave_number = jnp.mod(wave_number, extent)
    phase_angle = wave_number.astype(jnp.float32) * (2.0 * math.pi / extent)
    return jnp.cos(phase_angle), jnp.sin(phase_angle)


def block_form(peram_pair):
    peram_re = peram_pair[0]
    peram_im = peram_pair[1]
    top_half = jnp.concatenate([peram_re, peram_im], axis=1)
    bottom_half = jnp.concatenate([-peram_im, peram_re], axis=1)
    return jnp.concatenate([top_half, bottom_half], axis=0)


def reference(eigvecs, momenta, peram, graph):
    num_vec = eigvecs.shape[1]
    num_sites = eigvecs.shape[3]
    site_index = jnp.arange(num_sites, dtype=jnp.int32)
    cosine, sine = phase_tables(momenta, site_index, EXTENT)
    vec_re = eigvecs[0].astype(jnp.float32)
    vec_im = eigvecs[1].astype(jnp.float32)
    right_side = jnp.concatenate([
        jnp.concatenate([eigvecs[0], -eigvecs[1]], axis=1),
        jnp.concatenate([eigvecs[1], eigvecs[0]], axis=1)], axis=0).reshape(2 * num_vec, 6 * num_sites)

    def one_momentum(tables):
        cos_row, sin_row = tables
        left_re = vec_re * cos_row - vec_im * sin_row
        left_im = -(vec_re * sin_row + vec_im * cos_row)
        left_cat = jnp.concatenate([left_re, left_im], axis=1).astype(jnp.bfloat16).reshape(num_vec, 6 * num_sites)
        return lax.dot_general(left_cat, right_side, (((1,), (1,)), ((), ())), preferred_element_type=jnp.float32)

    elementals = lax.map(one_momentum, (cosine, sine))
    elemental = elementals.reshape(-1, 2 * num_vec).astype(jnp.bfloat16)
    blocks = jax.vmap(block_form)(peram)
    fanout = graph.shape[1]
    row_blocks = elemental.reshape(-1, 16, 2 * num_vec)
    owner_blocks = graph.reshape(-1, 16, fanout)

    def contract(pair):
        row_group, owners = pair
        first_blocks = blocks[owners].astype(jnp.float32)
        second_blocks = blocks[jnp.bitwise_xor(owners, 1)].astype(jnp.float32)
        sinks = jnp.einsum('ra,rkab->rkb', row_group.astype(jnp.float32), first_blocks).astype(jnp.bfloat16)
        return jnp.einsum('rka,rkba->rkb', sinks.astype(jnp.float32), second_blocks).astype(jnp.bfloat16)

    result = lax.map(contract, (row_blocks, owner_blocks))
    return result.reshape(-1, fanout, 2 * num_vec)
```

```python
import functools
import math

import jax
import jax.numpy as jnp
from jax import lax
from jax.experimental import pallas as pl
from jax.experimental.pallas import tpu as pltpu
from jax.sharding import PartitionSpec as P

EXTENT = 128


def partner(block, axis, bit):
    count = lax.axis_size(axis)
    route = []
    for low in range(count):
        high = low | 1 << bit
        if high != low and high < count:
            route += [(low, high), (high, low)]
    return lax.ppermute(block, axis, route)


def phase_tables(momenta, site_index, extent):
    coord_x = site_index % extent
    coord_y = site_index // extent % extent
    coord_z = site_index // (extent * extent)
    wave_number = (
        momenta[:, 0:1] * coord_x[None, :]
        + momenta[:, 1:2] * coord_y[None, :]
        + momenta[:, 2:3] * coord_z[None, :]
    )
    wave_number = jnp.mod(wave_number, extent)
    phase_angle = wave_number.astype(jnp.float32) * (2.0 * math.pi / extent)
    return (jnp.cos(phase_angle), jnp.sin(phase_angle))


def block_form(peram_pair):
    peram_re = peram_pair[0]
    peram_im = peram_pair[1]
    top_half = jnp.concatenate([peram_re, peram_im], axis=1)
    bottom_half = jnp.concatenate([-peram_im, peram_re], axis=1)
    return jnp.concatenate([top_half, bottom_half], axis=0)


def sink_product(arrived, block):
    return lax.dot_general(
        arrived, block, (((2,), (0,)), ((), ())), preferred_element_type=jnp.float32
    ).astype(jnp.bfloat16)


def adjoint_product(sinks, block):
    return lax.dot_general(
        sinks, block, (((2,), (1,)), ((), ())), preferred_element_type=jnp.float32
    ).astype(jnp.bfloat16)


def exchange_plan(eigvecs, momenta, peram, graph):
    num_vec = eigvecs.shape[1]
    local_sites = eigvecs.shape[3]
    spaces = lax.axis_size("space")
    position = lax.axis_index("space")
    site_index = position * local_sites + jnp.arange(local_sites, dtype=jnp.int32)
    cosine, sine = phase_tables(momenta, site_index, EXTENT)
    total_rows = cosine.shape[0] * num_vec
    rows_here = total_rows // spaces
    right_side = jnp.concatenate(
        [
            jnp.concatenate([eigvecs[0], -eigvecs[1]], axis=1),
            jnp.concatenate([eigvecs[1], eigvecs[0]], axis=1),
        ],
        axis=0,
    ).reshape(2 * num_vec, 6 * local_sites)
    row_index = jnp.arange(rows_here * lax.axis_size("space"), dtype=jnp.int32)
    vector_index = row_index % num_vec
    momentum_index = row_index // num_vec
    vec_re = jnp.take(eigvecs[0], vector_index, axis=0).astype(jnp.float32)
    vec_im = jnp.take(eigvecs[1], vector_index, axis=0).astype(jnp.float32)
    cos_rows = jnp.take(cosine, momentum_index, axis=0)[:, None, :]
    sin_rows = jnp.take(sine, momentum_index, axis=0)[:, None, :]
    left_re = vec_re * cos_rows - vec_im * sin_rows
    left_im = -(vec_re * sin_rows + vec_im * cos_rows)
    left_cat = (
        jnp.concatenate([left_re, left_im], axis=1)
        .astype(jnp.bfloat16)
        .reshape(rows_here * lax.axis_size("space"), 6 * local_sites)
    )
    summed = lax.psum_scatter(
        lax.dot_general(
            left_cat, right_side, (((1,), (1,)), ((), ())), preferred_element_type=jnp.float32
        ),
        "space",
        scatter_dimension=0,
        tiled=True,
    )
    elemental = summed.astype(jnp.bfloat16)
    fanout = graph.shape[1]
    capacity = max(2, 2 * rows_here * fanout // spaces)
    flat_owner = graph.reshape(-1)
    entries = flat_owner.shape[0]
    onehot = (flat_owner[:, None] == jnp.arange(spaces, dtype=jnp.int32)[None, :]).astype(jnp.int32)
    earlier = jnp.cumsum(onehot, axis=0) - onehot
    slot = jnp.sum(earlier * onehot, axis=1)
    source_row = jnp.arange(entries, dtype=jnp.int32) // fanout
    payload = jnp.take(elemental, source_row, axis=0)
    outgoing = (
        jnp.zeros((spaces, capacity, 2 * num_vec), jnp.bfloat16).at[flat_owner, slot].set(payload)
    )
    own_block = block_form(peram[0])
    partner_block = partner(own_block, "space", 0)
    sinks = sink_product(
        lax.all_to_all(outgoing, "space", split_axis=0, concat_axis=0, tiled=True), own_block
    )
    finished = adjoint_product(sinks, partner_block)
    returned = lax.all_to_all(finished, "space", split_axis=0, concat_axis=0, tiled=True)
    collected = returned[flat_owner, slot]
    return collected.reshape(rows_here, fanout, 2 * num_vec)


CORES = 2
PAIR = 2
VMEM_LIMIT = 40 * 1024 * 1024


def whole(space):
    return pl.BlockSpec(memory_space=space)


def nt_dot(left, right):
    return lax.dot_general(
        left, right, (((1,), (1,)), ((), ())), preferred_element_type=jnp.float32
    )


def nn_dot(left, right):
    return lax.dot_general(
        left, right, (((1,), (0,)), ((), ())), preferred_element_type=jnp.float32
    )


def product_kernel(core_ref, own_ref, other_ref, out_ref):
    @pl.when(core_ref[0] == 0)
    def _():
        out_ref[...] = (
            nt_dot(own_ref[0], other_ref[0]) + nt_dot(own_ref[1], other_ref[1])
        ).astype(out_ref.dtype)

    @pl.when(core_ref[0] != 0)
    def _():
        out_ref[...] = (
            nt_dot(other_ref[1], own_ref[0]) - nt_dot(other_ref[0], own_ref[1])
        ).astype(out_ref.dtype)


def partial_kernel(rows, chain, keep, place_ref, mom_ref, v_ref, out_ref, left_ref, right_ref):
    num_vec, sites = v_ref.shape[2], v_ref.shape[3]
    colours = v_ref.shape[1]
    zed, why, core = place_ref[0], place_ref[1], place_ref[2]
    position = (zed * PAIR + why) * CORES + core
    side = core if keep else 1 - core
    for c in range(colours):
        for part in range(2):
            column = pl.ds((part * colours + c) * sites, sites)
            right_ref[:num_vec, column] = v_ref[part, c]
            if part == 1:
                right_ref[num_vec:, column] = -v_ref[0, c]
            else:
                right_ref[num_vec:, column] = v_ref[1, c]
    site = position * sites + lax.broadcasted_iota(jnp.int32, (1, sites), 1)
    coord_x = site & (EXTENT - 1)
    coord_y = lax.div(site, EXTENT) & (EXTENT - 1)
    coord_z = lax.div(site, EXTENT * EXTENT)
    for shift in range(chain):
        for half in range(PAIR):
            target_z = lax.rem(zed + shift, chain)
            target_y = why if half else 1 - why
            first = ((target_z * PAIR + target_y) * CORES + side) * rows
            momentum = lax.div(first, num_vec)
            start = pl.multiple_of(lax.rem(first, num_vec), rows)
            wave = (
                mom_ref[momentum, 0] * coord_x
                + mom_ref[momentum, 1] * coord_y
                + mom_ref[momentum, 2] * coord_z
            ) & (EXTENT - 1)
            angle = wave.astype(jnp.float32) * (2.0 * math.pi / EXTENT)
            cosine, sine = jnp.cos(angle), jnp.sin(angle)
            place = pl.ds((half * chain + shift) * rows, rows)
            for c in range(colours):
                vec_re = v_ref[0, c, pl.ds(start, rows), :].astype(jnp.float32)
                vec_im = v_ref[1, c, pl.ds(start, rows), :].astype(jnp.float32)
                left_ref[place, pl.ds(c * sites, sites)] = (
                    vec_re * cosine - vec_im * sine
                ).astype(jnp.bfloat16)
                left_ref[place, pl.ds((colours + c) * sites, sites)] = (
                    vec_re * sine + vec_im * cosine
                ).astype(jnp.bfloat16)
    out_ref[...] = nt_dot(left_ref[...], right_ref[...]).astype(out_ref.dtype)


def partial_rows(rows, chain, keep, place, momenta, vectors):
    _, colours, num_vec, sites = vectors.shape
    depth = 2 * colours * sites
    height = PAIR * chain * rows
    dtype = jnp.float32 if keep else jnp.bfloat16
    return pl.pallas_call(
        functools.partial(partial_kernel, rows, chain, keep),
        out_shape=jax.ShapeDtypeStruct((height, 2 * num_vec), dtype),
        in_specs=[whole(pltpu.SMEM), whole(pltpu.SMEM), whole(pltpu.VMEM)],
        out_specs=whole(pltpu.VMEM),
        scratch_shapes=[
            pltpu.VMEM((height, depth), jnp.bfloat16),
            pltpu.VMEM((2 * num_vec, depth), jnp.bfloat16),
        ],
        compiler_params=pltpu.CompilerParams(vmem_limit_bytes=VMEM_LIMIT),
        cost_estimate=pl.CostEstimate(
            flops=2 * height * depth * 2 * num_vec,
            bytes_accessed=vectors.size * 2 + height * 2 * num_vec * 4,
            transcendentals=0,
        ),
    )(place, momenta, vectors)


def owner_products(core, stacked, own, other, even_ref, odd_ref):
    rows = even_ref.shape[0]
    num_vec = own.shape[1]
    for direct, ref in ((True, even_ref), (False, odd_ref)):
        product = nn_dot if direct else nt_dot
        by_own, by_other = product(stacked, own), product(stacked, other)
        by_real = jnp.where(core == 0, by_own, by_other)
        by_imag = jnp.where(core == 0, by_other, by_own)
        if direct:
            real = by_real[:rows] - by_imag[rows:]
            imag = by_imag[:rows] + by_real[rows:]
        else:
            real = by_real[:rows] + by_imag[rows:]
            imag = by_real[rows:] - by_imag[:rows]
        ref[:, :num_vec] = real.astype(jnp.bfloat16)
        ref[:, num_vec:] = imag.astype(jnp.bfloat16)


def contract_kernel(slots, arrivals, group, core_ref, *refs):
    terms, refs = refs[:arrivals], refs[arrivals:]
    own, refs = refs[:slots], refs[slots:]
    other, refs = refs[:slots], refs[slots:]
    pick_ref, out_ref, full_ref = refs
    rows, fanout, width = out_ref.shape
    num_vec = width // 2
    total = terms[0][...].astype(jnp.float32)
    for term in terms[1:]:
        total = total + term[...].astype(jnp.float32)
    elemental = total.astype(jnp.bfloat16)
    stacked = jnp.concatenate([elemental[:, :num_vec], elemental[:, num_vec:]], axis=0)
    for slot in range(slots):
        owner_products(
            core_ref[0],
            stacked,
            own[slot][...],
            other[slot][...],
            full_ref.at[2 * slot],
            full_ref.at[2 * slot + 1],
        )
    for block in range(rows // group):
        table = full_ref[:, pl.ds(block * group, group), :].reshape(2 * slots * group, width)
        picked = nn_dot(pick_ref[pl.ds(block * group * fanout, group * fanout), :], table)
        out_ref[pl.ds(block * group, group)] = picked.astype(jnp.bfloat16).reshape(
            group, fanout, width
        )


def gather_plan(eigvecs, momenta, peram, graph):
    num_vec = eigvecs.shape[1]
    spaces = lax.axis_size("space")
    chain = spaces // (PAIR * CORES)
    rows = momenta.shape[0] * num_vec // spaces
    fanout = graph.shape[1]
    here = lax.axis_index("space")
    zed, why, core = here // (PAIR * CORES), here // CORES % PAIR, here % CORES
    place = jnp.stack([zed, why, core]).astype(jnp.int32)
    core_at = place[2:]

    def index(z, y, c):
        return (z * PAIR + y) * CORES + c

    def send(block, moves):
        route = [
            (index(a, y, c), index(b, y, c))
            for a, b in moves
            for y in range(PAIR)
            for c in range(CORES)
        ]
        return lax.ppermute(block, "space", route)

    def across(block):
        return lax.ppermute(block, "space", [(i, i ^ CORES) for i in range(spaces)])

    def swap(block):
        return lax.ppermute(block, "space", [(i, i ^ 1) for i in range(spaces)])

    with jax.named_scope("matrices"):
        mine = peram[0]
        own = pl.pallas_call(
            product_kernel,
            out_shape=jax.ShapeDtypeStruct((num_vec, num_vec), jnp.bfloat16),
            in_specs=[whole(pltpu.SMEM), whole(pltpu.VMEM), whole(pltpu.VMEM)],
            out_specs=whole(pltpu.VMEM),
            compiler_params=pltpu.CompilerParams(vmem_limit_bytes=VMEM_LIMIT),
            cost_estimate=pl.CostEstimate(
                flops=4 * num_vec**3, bytes_accessed=10 * num_vec**2, transcendentals=0
            ),
        )(core_at, mine, swap(mine))
    inner = (zed > 0) & (zed < chain - 1)
    with jax.named_scope("spread"):
        near = send(own, [(0, 1), (1, 0), (2, 3), (3, 2)])
        middle = send(own, [(1, 2), (2, 1)])
        outward = send(middle, [(1, 0), (2, 3)])
        third = jnp.where(inner, middle, outward)
        crossing = send(near, [(1, 2), (2, 1)])
        last = send(crossing, [(1, 0), (2, 3)])
        fourth = jnp.where(inner, crossing, last)
        held = [own, across(own), near, across(near), third, across(third), fourth, across(fourth)]
        swapped = [swap(block) for block in held]
        columns = []
        for step in range(chain):
            source = jnp.asarray(SOURCES[step], jnp.int32)[zed]
            for other in range(PAIR):
                chip = source * PAIR + (why ^ other)
                columns += [chip * CORES, chip * CORES + 1]
    with jax.named_scope("elementals"):
        vectors = jnp.transpose(eigvecs, (0, 2, 1, 3))
        away = partial_rows(rows, chain, False, place, momenta, vectors)
        arrived = swap(away)
        kept = partial_rows(rows, chain, True, place, momenta, vectors)
        half = chain * rows
        outgoing = (kept[:half] + arrived[:half].astype(jnp.float32)).astype(jnp.bfloat16)
        crossed = across(outgoing)
        summed = kept[half:] + arrived[half:].astype(jnp.float32) + crossed.astype(jnp.float32)
        terms = [summed[:rows]]
        for shift in range(1, chain):
            chunk = summed[shift * rows : (shift + 1) * rows].astype(jnp.bfloat16)
            terms.append(send(chunk, [(z, (z + shift) % chain) for z in range(chain)]))
    with jax.named_scope("pick"):
        group = 16
        owner_of = jnp.repeat(jnp.stack(columns), group)
        row_of = jnp.arange(rows * fanout, dtype=jnp.int32) // fanout % group
        place_of = jnp.arange(spaces * group, dtype=jnp.int32) % group
        pick = (
            (graph.reshape(-1)[:, None] == owner_of[None, :])
            & (row_of[:, None] == place_of[None, :])
        ).astype(jnp.bfloat16)
    with jax.named_scope("contract"):
        slots = len(held)
        return pl.pallas_call(
            functools.partial(contract_kernel, slots, len(terms), group),
            out_shape=jax.ShapeDtypeStruct((rows, fanout, 2 * num_vec), jnp.bfloat16),
            in_specs=[whole(pltpu.SMEM)] + [whole(pltpu.VMEM)] * (len(terms) + 2 * slots + 1),
            out_specs=whole(pltpu.VMEM),
            scratch_shapes=[pltpu.VMEM((2 * slots, rows, 2 * num_vec), jnp.bfloat16)],
            compiler_params=pltpu.CompilerParams(vmem_limit_bytes=VMEM_LIMIT),
            cost_estimate=pl.CostEstimate(
                flops=16 * slots * rows * num_vec**2,
                bytes_accessed=4 * slots * num_vec**2,
                transcendentals=0,
            ),
        )(core_at, *terms, *held, *swapped, pick)


SOURCES = ((0, 1, 2, 3), (1, 0, 3, 2), (2, 2, 1, 1), (3, 3, 0, 0))


def on_device(eigvecs, momenta, peram, graph):
    num_vec = eigvecs.shape[1]
    spaces = lax.axis_size("space")
    rows = momenta.shape[0] * num_vec // spaces
    if spaces == CORES * PAIR * len(SOURCES) and num_vec % rows == 0 and rows % 16 == 0:
        return gather_plan(eigvecs, momenta, peram, graph)
    return exchange_plan(eigvecs, momenta, peram, graph)


def solution(mesh):
    placed = (
        P(None, None, None, ("groups", "space")),
        P(),
        P(("groups", "space"), None, None, None),
        P(("groups", "space"), None),
    )
    return jax.shard_map(
        on_device,
        mesh=mesh,
        in_specs=placed,
        out_specs=P(("groups", "space"), None, None),
        check_vma=False,
    )
```

```python
import functools
import math

import jax
import jax.numpy as jnp
from jax import lax
from jax.experimental import pallas as pl
from jax.experimental.pallas import tpu as pltpu
from jax.sharding import PartitionSpec as P

EXTENT = 128


def partner(block, axis, bit):
    count = lax.axis_size(axis)
    route = []
    for low in range(count):
        high = low | 1 << bit
        if high != low and high < count:
            route += [(low, high), (high, low)]
    return lax.ppermute(block, axis, route)


def phase_tables(momenta, site_index, extent):
    coord_x = site_index % extent
    coord_y = site_index // extent % extent
    coord_z = site_index // (extent * extent)
    wave_number = (
        momenta[:, 0:1] * coord_x[None, :]
        + momenta[:, 1:2] * coord_y[None, :]
        + momenta[:, 2:3] * coord_z[None, :]
    )
    wave_number = jnp.mod(wave_number, extent)
    phase_angle = wave_number.astype(jnp.float32) * (2.0 * math.pi / extent)
    return (jnp.cos(phase_angle), jnp.sin(phase_angle))


def block_form(peram_pair):
    peram_re = peram_pair[0]
    peram_im = peram_pair[1]
    top_half = jnp.concatenate([peram_re, peram_im], axis=1)
    bottom_half = jnp.concatenate([-peram_im, peram_re], axis=1)
    return jnp.concatenate([top_half, bottom_half], axis=0)


def sink_product(arrived, block):
    return lax.dot_general(
        arrived, block, (((2,), (0,)), ((), ())), preferred_element_type=jnp.float32
    ).astype(jnp.bfloat16)


def adjoint_product(sinks, block):
    return lax.dot_general(
        sinks, block, (((2,), (1,)), ((), ())), preferred_element_type=jnp.float32
    ).astype(jnp.bfloat16)


def exchange_plan(eigvecs, momenta, peram, graph):
    num_vec = eigvecs.shape[1]
    local_sites = eigvecs.shape[3]
    spaces = lax.axis_size("space")
    position = lax.axis_index("space")
    site_index = position * local_sites + jnp.arange(local_sites, dtype=jnp.int32)
    cosine, sine = phase_tables(momenta, site_index, EXTENT)
    total_rows = cosine.shape[0] * num_vec
    rows_here = total_rows // spaces
    right_side = jnp.concatenate(
        [
            jnp.concatenate([eigvecs[0], -eigvecs[1]], axis=1),
            jnp.concatenate([eigvecs[1], eigvecs[0]], axis=1),
        ],
        axis=0,
    ).reshape(2 * num_vec, 6 * local_sites)
    row_index = jnp.arange(rows_here * lax.axis_size("space"), dtype=jnp.int32)
    vector_index = row_index % num_vec
    momentum_index = row_index // num_vec
    vec_re = jnp.take(eigvecs[0], vector_index, axis=0).astype(jnp.float32)
    vec_im = jnp.take(eigvecs[1], vector_index, axis=0).astype(jnp.float32)
    cos_rows = jnp.take(cosine, momentum_index, axis=0)[:, None, :]
    sin_rows = jnp.take(sine, momentum_index, axis=0)[:, None, :]
    left_re = vec_re * cos_rows - vec_im * sin_rows
    left_im = -(vec_re * sin_rows + vec_im * cos_rows)
    left_cat = (
        jnp.concatenate([left_re, left_im], axis=1)
        .astype(jnp.bfloat16)
        .reshape(rows_here * lax.axis_size("space"), 6 * local_sites)
    )
    summed = lax.psum_scatter(
        lax.dot_general(
            left_cat, right_side, (((1,), (1,)), ((), ())), preferred_element_type=jnp.float32
        ),
        "space",
        scatter_dimension=0,
        tiled=True,
    )
    elemental = summed.astype(jnp.bfloat16)
    fanout = graph.shape[1]
    capacity = max(2, 2 * rows_here * fanout // spaces)
    flat_owner = graph.reshape(-1)
    entries = flat_owner.shape[0]
    onehot = (flat_owner[:, None] == jnp.arange(spaces, dtype=jnp.int32)[None, :]).astype(jnp.int32)
    earlier = jnp.cumsum(onehot, axis=0) - onehot
    slot = jnp.sum(earlier * onehot, axis=1)
    source_row = jnp.arange(entries, dtype=jnp.int32) // fanout
    payload = jnp.take(elemental, source_row, axis=0)
    outgoing = (
        jnp.zeros((spaces, capacity, 2 * num_vec), jnp.bfloat16).at[flat_owner, slot].set(payload)
    )
    own_block = block_form(peram[0])
    partner_block = partner(own_block, "space", 0)
    sinks = sink_product(
        lax.all_to_all(outgoing, "space", split_axis=0, concat_axis=0, tiled=True), own_block
    )
    finished = adjoint_product(sinks, partner_block)
    returned = lax.all_to_all(finished, "space", split_axis=0, concat_axis=0, tiled=True)
    collected = returned[flat_owner, slot]
    return collected.reshape(rows_here, fanout, 2 * num_vec)


CORES = 2
PAIR = 2
VMEM_LIMIT = 20 * 1024 * 1024


def whole(space):
    return pl.BlockSpec(memory_space=space)


def nt_dot(left, right):
    return lax.dot_general(
        left, right, (((1,), (1,)), ((), ())), preferred_element_type=jnp.float32
    )


def nn_dot(left, right):
    return lax.dot_general(
        left, right, (((1,), (0,)), ((), ())), preferred_element_type=jnp.float32
    )


def product_kernel(flip, core_ref, own_ref, other_ref, after_ref, out_ref):
    def real(even, odd):
        out_ref[...] = (nt_dot(even[0], odd[0]) + nt_dot(even[1], odd[1])).astype(out_ref.dtype)

    def imag(even, odd):
        out_ref[...] = (nt_dot(even[1], odd[0]) - nt_dot(even[0], odd[1])).astype(out_ref.dtype)

    first, second = (imag, real) if flip else (real, imag)

    @pl.when(core_ref[0] == 0)
    def _():
        first(own_ref, other_ref)

    @pl.when(core_ref[0] != 0)
    def _():
        second(other_ref, own_ref)


def partial_kernel(rows, chain, stay, place_ref, mom_ref, v_ref, *refs):
    away_ref, keep_ref, left_ref, right_ref, cos_ref, sin_ref = refs[-6:]
    num_vec, sites = v_ref.shape[2], v_ref.shape[3]
    colours, momenta = v_ref.shape[1], mom_ref.shape[0]
    height = chain * rows
    zed, why, core = place_ref[0], place_ref[1], place_ref[2]
    position = (zed * PAIR + why) * CORES + core
    target_y = why if stay else 1 - why
    for part in range(2):
        for c in range(colours):
            right_ref[pl.ds(part * num_vec, num_vec), pl.ds(c * sites, sites)] = v_ref[part, c]
    site = position * sites + lax.broadcasted_iota(jnp.int32, (momenta, sites), 1)
    coord_x = site & (EXTENT - 1)
    coord_y = lax.div(site, EXTENT) & (EXTENT - 1)
    coord_z = lax.div(site, EXTENT * EXTENT)
    which = lax.broadcasted_iota(jnp.int32, (momenta, sites), 0)
    wave = jnp.zeros((momenta, sites), jnp.int32)
    for q in range(momenta):
        turned = mom_ref[q, 0] * coord_x + mom_ref[q, 1] * coord_y + mom_ref[q, 2] * coord_z
        wave = jnp.where(which == q, turned & (EXTENT - 1), wave)
    angle = wave.astype(jnp.float32) * (2.0 * math.pi / EXTENT)
    cos_ref[...] = jnp.cos(angle)
    sin_ref[...] = jnp.sin(angle)
    for keep, out_ref in ((False, away_ref), (True, keep_ref)):
        side = core if keep else 1 - core
        base = keep * 2 * height
        for turn in range(chain):
            target_z = lax.rem(zed + turn, chain)
            first = ((target_z * PAIR + target_y) * CORES + side) * rows
            momentum = lax.div(first, num_vec)
            start = pl.multiple_of(lax.rem(first, num_vec), rows)
            cosine, sine = cos_ref[pl.ds(momentum, 1), :], sin_ref[pl.ds(momentum, 1), :]
            for c in range(colours):
                vec_re = v_ref[0, c, pl.ds(start, rows), :].astype(jnp.float32)
                vec_im = v_ref[1, c, pl.ds(start, rows), :].astype(jnp.float32)
                column = pl.ds(c * sites, sites)
                left_ref[pl.ds(base + turn * rows, rows), column] = (
                    vec_re * cosine - vec_im * sine
                ).astype(jnp.bfloat16)
                left_ref[pl.ds(base + height + turn * rows, rows), column] = (
                    vec_re * sine + vec_im * cosine
                ).astype(jnp.bfloat16)
        both = nt_dot(left_ref[pl.ds(base, 2 * height), :], right_ref[...])
        out_ref[:, :num_vec] = (both[:height, :num_vec] + both[height:, num_vec:]).astype(out_ref.dtype)
        out_ref[:, num_vec:] = (both[:height, num_vec:] - both[height:, :num_vec]).astype(out_ref.dtype)


def partial_rows(rows, chain, stay, place, momenta, vectors, *after):
    _, colours, num_vec, sites = vectors.shape
    depth = colours * sites
    height = chain * rows
    return pl.pallas_call(
        functools.partial(partial_kernel, rows, chain, stay),
        out_shape=(
            jax.ShapeDtypeStruct((height, 2 * num_vec), jnp.bfloat16),
            jax.ShapeDtypeStruct((height, 2 * num_vec), jnp.float32),
        ),
        in_specs=[whole(pltpu.SMEM), whole(pltpu.SMEM), whole(pltpu.VMEM)] + [whole(pl.ANY)] * len(after),
        out_specs=(whole(pltpu.VMEM), whole(pltpu.VMEM)),
        scratch_shapes=[
            pltpu.VMEM((4 * height, depth), jnp.bfloat16),
            pltpu.VMEM((2 * num_vec, depth), jnp.bfloat16),
            pltpu.VMEM((momenta.shape[0], sites), jnp.float32),
            pltpu.VMEM((momenta.shape[0], sites), jnp.float32),
        ],
        compiler_params=pltpu.CompilerParams(vmem_limit_bytes=VMEM_LIMIT),
        cost_estimate=pl.CostEstimate(flops=16 * height * depth * num_vec, bytes_accessed=vectors.size * 2 + height * num_vec * 12, transcendentals=0),
    )(place, momenta, vectors, *after)


def total_kernel(count, *refs):
    total = refs[0][...].astype(jnp.float32)
    for term in refs[1:count]:
        total = total + term[...].astype(jnp.float32)
    refs[-1][...] = total.astype(jnp.bfloat16)


def total(terms, *passed):
    def kernel(*refs):
        count = len(terms)
        total_kernel(count, *refs[:count], refs[count + len(passed)])

    return pl.pallas_call(
        kernel,
        out_shape=(jax.ShapeDtypeStruct(terms[0].shape, jnp.bfloat16),)
        + tuple(jax.ShapeDtypeStruct(block.shape, block.dtype) for block in passed),
        in_specs=[whole(pltpu.VMEM)] * len(terms) + [whole(pl.ANY)] * len(passed),
        out_specs=(whole(pltpu.VMEM),) + (whole(pl.ANY),) * len(passed),
        input_output_aliases={len(terms) + i: 1 + i for i in range(len(passed))},
        compiler_params=pltpu.CompilerParams(vmem_limit_bytes=VMEM_LIMIT),
        cost_estimate=pl.CostEstimate(flops=4 * terms[0].size, bytes_accessed=10 * terms[0].size, transcendentals=0),
    )(*terms, *passed)


def owner_products(core, stacked, own, other, even_ref, odd_ref):
    rows = even_ref.shape[0]
    num_vec = own.shape[1]
    for direct, ref in ((True, even_ref), (False, odd_ref)):
        product = nn_dot if direct else nt_dot
        by_own, by_other = product(stacked, own), product(stacked, other)
        by_real = jnp.where(core == 0, by_own, by_other)
        by_imag = jnp.where(core == 0, by_other, by_own)
        if direct:
            real = by_real[:rows] - by_imag[rows:]
            imag = by_imag[:rows] + by_real[rows:]
        else:
            real = by_real[:rows] + by_imag[rows:]
            imag = by_real[rows:] - by_imag[:rows]
        ref[:, :num_vec] = real.astype(jnp.bfloat16)
        ref[:, num_vec:] = imag.astype(jnp.bfloat16)


def rows_kernel(slots, arrivals, core_ref, *refs):
    terms, refs = refs[:arrivals], refs[arrivals:]
    own, other = refs[:slots], refs[slots : 2 * slots]
    stacked_ref, full_ref = refs[2 * slots :]
    num_vec = terms[0].shape[1] // 2
    rows = stacked_ref.shape[0] // 2
    total = 0.0
    for term in terms:
        for at in range(0, term.shape[0], rows):
            total = total + term[pl.ds(at, rows), :].astype(jnp.float32)
    elemental = total.astype(jnp.bfloat16)
    stacked = jnp.concatenate([elemental[:, :num_vec], elemental[:, num_vec:]], axis=0)
    stacked_ref[...] = stacked
    for slot in range(slots):
        owner_products(
            core_ref[0],
            stacked,
            own[slot][...],
            other[slot][...],
            full_ref.at[2 * slot],
            full_ref.at[2 * slot + 1],
        )


def pick_kernel(slots, group, core_ref, stacked_ref, first_ref, *refs):
    own, other = refs[:slots], refs[slots : 2 * slots]
    pick_ref, out_ref, last_ref = refs[2 * slots :]
    rows, fanout, width = out_ref.shape
    stacked = stacked_ref[...]
    for slot in range(slots):
        owner_products(
            core_ref[0],
            stacked,
            own[slot][...],
            other[slot][...],
            last_ref.at[2 * slot],
            last_ref.at[2 * slot + 1],
        )
    for block in range(rows // group):
        there = pl.ds(block * group, group)
        table = jnp.concatenate(
            [
                first_ref[:, there, :].reshape(first_ref.shape[0] * group, width),
                last_ref[:, there, :].reshape(2 * slots * group, width),
            ],
            axis=0,
        )
        picked = nn_dot(pick_ref[pl.ds(block * group * fanout, group * fanout), :], table)
        out_ref[there] = picked.astype(jnp.bfloat16).reshape(group, fanout, width)


def named(name, step):
    with jax.named_scope(name):
        return step()


def gather_plan(eigvecs, momenta, peram, graph):
    num_vec = eigvecs.shape[1]
    spaces = lax.axis_size("space")
    chain = spaces // (PAIR * CORES)
    rows = momenta.shape[0] * num_vec // spaces
    fanout = graph.shape[1]
    here = lax.axis_index("space")
    zed, why, core = here // (PAIR * CORES), here // CORES % PAIR, here % CORES
    place = jnp.stack([zed, why, core]).astype(jnp.int32)
    core_at = place[2:]

    def index(z, y, c):
        return (z * PAIR + y) * CORES + c

    def send(block, moves):
        route = [
            (index(a, y, c), index(b, y, c))
            for a, b in moves
            for y in range(PAIR)
            for c in range(CORES)
        ]
        return lax.ppermute(block, "space", route)

    def across(block):
        return lax.ppermute(block, "space", [(i, i ^ CORES) for i in range(spaces)])

    def swap(block):
        return lax.ppermute(block, "space", [(i, i ^ 1) for i in range(spaces)])

    with jax.named_scope("matrices"):
        mine = peram[0]
        theirs = named("swapP", lambda: swap(mine))

        def matrix(flip, after):
            return pl.pallas_call(
                functools.partial(product_kernel, flip),
                out_shape=jax.ShapeDtypeStruct((num_vec, num_vec), jnp.bfloat16),
                in_specs=[whole(pltpu.SMEM), whole(pltpu.VMEM), whole(pltpu.VMEM), whole(pl.ANY)],
                out_specs=whole(pltpu.VMEM),
                compiler_params=pltpu.CompilerParams(vmem_limit_bytes=VMEM_LIMIT),
                cost_estimate=pl.CostEstimate(flops=4 * num_vec**3, bytes_accessed=10 * num_vec**2, transcendentals=0),
            )(core_at, mine, theirs, after)

        own = matrix(False, core_at)
    inner = (zed > 0) & (zed < chain - 1)
    half = chain * rows
    with jax.named_scope("elementals"):
        vectors = jnp.transpose(eigvecs, (0, 2, 1, 3))
        away_cross, kept_cross = partial_rows(rows, chain, False, place, momenta, vectors)
        away_stay, kept_stay = partial_rows(rows, chain, True, place, momenta, vectors, own)
        got_cross = named("swapA", lambda: swap(away_cross))
    with jax.named_scope("spread"):
        near = named("near", lambda: send(own, [(0, 1), (1, 0), (2, 3), (3, 2)]))
        middle = named("middle", lambda: send(own, [(1, 2), (2, 1)]))
        beside = named("beside", lambda: across(own))
    with jax.named_scope("elementals"):
        outgoing, near, middle, away_stay = total([kept_cross, got_cross], near, middle, away_stay)
        crossed = named("RSy", lambda: across(outgoing))
        got_stay = named("swapB", lambda: swap(away_stay))
    with jax.named_scope("spread"):
        third_in = named("third_in", lambda: send(near, [(1, 2), (2, 1)]))
        third_out = named("third_out", lambda: send(middle, [(1, 0), (2, 3)]))
        ends = named("ends", lambda: send(third_in, [(1, 0), (2, 3)]))
        twin = matrix(True, outgoing)
        third = jnp.where(inner, third_in, third_out)
        fourth = jnp.where(inner, middle, ends)
        twin_beside, twin_near = [named("swE", lambda: swap(block)) for block in (beside, near)]
    with jax.named_scope("elementals"):
        summed, near, third, twin, twin_beside, twin_near = total(
            [kept_stay, got_stay, crossed], near, third, twin, twin_beside, twin_near
        )
    with jax.named_scope("spread"):
        beside_near, beside_third = [named("Y", lambda: across(block)) for block in (near, third)]
        early = [own, beside, near, third, beside_near, beside_third]
        early_twins = [twin, twin_beside, twin_near]
        early_twins += [named("swE", lambda: swap(block)) for block in (third, beside_near, beside_third)]
        late = [fourth, named("Yf", lambda: across(fourth))]
        late_twins = [named("swL", lambda: swap(block)) for block in late]
    with jax.named_scope("elementals"):
        terms = [summed[:rows]]
        for shift in range(1, chain):
            moves = [(z, (z + shift) % chain) for z in range(chain)]
            chunk = summed[shift * rows : (shift + 1) * rows]
            terms.append(named("RSz", lambda: send(chunk, moves)))
    with jax.named_scope("pick"):
        group = 16
        near_z, third_z, fourth_z = zed ^ 1, (zed + 2) % chain, chain - 1 - zed
        chips = []
        for z, y in (
            (zed, why),
            (zed, 1 - why),
            (near_z, why),
            (third_z, why),
            (near_z, 1 - why),
            (third_z, 1 - why),
            (fourth_z, why),
            (fourth_z, 1 - why),
        ):
            chips.append(z * PAIR + y)
        columns = jnp.arange(spaces * group, dtype=jnp.int32)
        slot_of = columns // (CORES * group)
        owner_of = columns // group % CORES
        for slot, chip in enumerate(chips):
            owner_of = owner_of + jnp.where(slot_of == slot, chip * CORES, 0)
        row_of = jnp.arange(rows * fanout, dtype=jnp.int32) // fanout % group
        pick = (
            (graph.reshape(-1)[:, None] == owner_of[None, :])
            & (row_of[:, None] == (columns % group)[None, :])
        ).astype(jnp.bfloat16)
    with jax.named_scope("contract"):
        slots = len(early)
        stacked, first = pl.pallas_call(
            functools.partial(rows_kernel, slots, len(terms)),
            out_shape=(
                jax.ShapeDtypeStruct((2 * rows, num_vec), jnp.bfloat16),
                jax.ShapeDtypeStruct((2 * slots, rows, 2 * num_vec), jnp.bfloat16),
            ),
            in_specs=[whole(pltpu.SMEM)] + [whole(pltpu.VMEM)] * (len(terms) + 2 * slots),
            out_specs=(whole(pltpu.VMEM), whole(pltpu.VMEM)),
            compiler_params=pltpu.CompilerParams(vmem_limit_bytes=VMEM_LIMIT),
            cost_estimate=pl.CostEstimate(flops=16 * slots * rows * num_vec**2, bytes_accessed=8 * slots * num_vec**2, transcendentals=0),
        )(core_at, *terms, *early, *early_twins)
        slots = len(late)
        return pl.pallas_call(
            functools.partial(pick_kernel, slots, group),
            out_shape=jax.ShapeDtypeStruct((rows, fanout, 2 * num_vec), jnp.bfloat16),
            in_specs=[whole(pltpu.SMEM)] + [whole(pltpu.VMEM)] * (2 + 2 * slots + 1),
            out_specs=whole(pltpu.VMEM),
            scratch_shapes=[pltpu.VMEM((2 * slots, rows, 2 * num_vec), jnp.bfloat16)],
            compiler_params=pltpu.CompilerParams(vmem_limit_bytes=VMEM_LIMIT),
            cost_estimate=pl.CostEstimate(flops=16 * slots * rows * num_vec**2, bytes_accessed=8 * slots * num_vec**2, transcendentals=0),
        )(core_at, stacked, first, *late, *late_twins, pick)


LINE = 4


def on_device(eigvecs, momenta, peram, graph):
    num_vec = eigvecs.shape[1]
    spaces = lax.axis_size("space")
    rows = momenta.shape[0] * num_vec // spaces
    if spaces == CORES * PAIR * LINE and num_vec % rows == 0 and rows % 16 == 0:
        return gather_plan(eigvecs, momenta, peram, graph)
    return exchange_plan(eigvecs, momenta, peram, graph)


def solution(mesh):
    placed = (
        P(None, None, None, ("groups", "space")),
        P(),
        P(("groups", "space"), None, None, None),
        P(("groups", "space"), None),
    )
    return jax.shard_map(
        on_device,
        mesh=mesh,
        in_specs=placed,
        out_specs=P(("groups", "space"), None, None),
        check_vma=False,
    )
```

```python
import functools
import math

import jax
import jax.numpy as jnp
from jax import lax
from jax.experimental import pallas as pl
from jax.experimental.pallas import tpu as pltpu
from jax.sharding import PartitionSpec as P

EXTENT = 128


def partner(block, axis, bit):
    count = lax.axis_size(axis)
    route = []
    for low in range(count):
        high = low | 1 << bit
        if high != low and high < count:
            route += [(low, high), (high, low)]
    return lax.ppermute(block, axis, route)


def phase_tables(momenta, site_index, extent):
    coord_x = site_index % extent
    coord_y = site_index // extent % extent
    coord_z = site_index // (extent * extent)
    wave_number = (
        momenta[:, 0:1] * coord_x[None, :]
        + momenta[:, 1:2] * coord_y[None, :]
        + momenta[:, 2:3] * coord_z[None, :]
    )
    wave_number = jnp.mod(wave_number, extent)
    phase_angle = wave_number.astype(jnp.float32) * (2.0 * math.pi / extent)
    return (jnp.cos(phase_angle), jnp.sin(phase_angle))


def block_form(peram_pair):
    peram_re = peram_pair[0]
    peram_im = peram_pair[1]
    top_half = jnp.concatenate([peram_re, peram_im], axis=1)
    bottom_half = jnp.concatenate([-peram_im, peram_re], axis=1)
    return jnp.concatenate([top_half, bottom_half], axis=0)


def sink_product(arrived, block):
    return lax.dot_general(
        arrived, block, (((2,), (0,)), ((), ())), preferred_element_type=jnp.float32
    ).astype(jnp.bfloat16)


def adjoint_product(sinks, block):
    return lax.dot_general(
        sinks, block, (((2,), (1,)), ((), ())), preferred_element_type=jnp.float32
    ).astype(jnp.bfloat16)


def exchange_plan(eigvecs, momenta, peram, graph):
    num_vec = eigvecs.shape[1]
    local_sites = eigvecs.shape[3]
    spaces = lax.axis_size("space")
    position = lax.axis_index("space")
    site_index = position * local_sites + jnp.arange(local_sites, dtype=jnp.int32)
    cosine, sine = phase_tables(momenta, site_index, EXTENT)
    total_rows = cosine.shape[0] * num_vec
    rows_here = total_rows // spaces
    right_side = jnp.concatenate(
        [
            jnp.concatenate([eigvecs[0], -eigvecs[1]], axis=1),
            jnp.concatenate([eigvecs[1], eigvecs[0]], axis=1),
        ],
        axis=0,
    ).reshape(2 * num_vec, 6 * local_sites)
    row_index = jnp.arange(rows_here * lax.axis_size("space"), dtype=jnp.int32)
    vector_index = row_index % num_vec
    momentum_index = row_index // num_vec
    vec_re = jnp.take(eigvecs[0], vector_index, axis=0).astype(jnp.float32)
    vec_im = jnp.take(eigvecs[1], vector_index, axis=0).astype(jnp.float32)
    cos_rows = jnp.take(cosine, momentum_index, axis=0)[:, None, :]
    sin_rows = jnp.take(sine, momentum_index, axis=0)[:, None, :]
    left_re = vec_re * cos_rows - vec_im * sin_rows
    left_im = -(vec_re * sin_rows + vec_im * cos_rows)
    left_cat = (
        jnp.concatenate([left_re, left_im], axis=1)
        .astype(jnp.bfloat16)
        .reshape(rows_here * lax.axis_size("space"), 6 * local_sites)
    )
    summed = lax.psum_scatter(
        lax.dot_general(
            left_cat, right_side, (((1,), (1,)), ((), ())), preferred_element_type=jnp.float32
        ),
        "space",
        scatter_dimension=0,
        tiled=True,
    )
    elemental = summed.astype(jnp.bfloat16)
    fanout = graph.shape[1]
    capacity = max(2, 2 * rows_here * fanout // spaces)
    flat_owner = graph.reshape(-1)
    entries = flat_owner.shape[0]
    onehot = (flat_owner[:, None] == jnp.arange(spaces, dtype=jnp.int32)[None, :]).astype(jnp.int32)
    earlier = jnp.cumsum(onehot, axis=0) - onehot
    slot = jnp.sum(earlier * onehot, axis=1)
    source_row = jnp.arange(entries, dtype=jnp.int32) // fanout
    payload = jnp.take(elemental, source_row, axis=0)
    outgoing = (
        jnp.zeros((spaces, capacity, 2 * num_vec), jnp.bfloat16).at[flat_owner, slot].set(payload)
    )
    own_block = block_form(peram[0])
    partner_block = partner(own_block, "space", 0)
    sinks = sink_product(
        lax.all_to_all(outgoing, "space", split_axis=0, concat_axis=0, tiled=True), own_block
    )
    finished = adjoint_product(sinks, partner_block)
    returned = lax.all_to_all(finished, "space", split_axis=0, concat_axis=0, tiled=True)
    collected = returned[flat_owner, slot]
    return collected.reshape(rows_here, fanout, 2 * num_vec)


CORES = 2
PAIR = 2
VMEM_LIMIT = 20 * 1024 * 1024


def whole(space):
    return pl.BlockSpec(memory_space=space)


def nt_dot(left, right):
    return lax.dot_general(
        left, right, (((1,), (1,)), ((), ())), preferred_element_type=jnp.float32
    )


def nn_dot(left, right):
    return lax.dot_general(
        left, right, (((1,), (0,)), ((), ())), preferred_element_type=jnp.float32
    )


def product_kernel(flip, copies, waits, core_ref, own_ref, other_ref, *refs):
    outs = refs[waits : waits + copies]

    def real(even, odd):
        value = nt_dot(even[0], odd[0]) + nt_dot(even[1], odd[1])
        for out_ref in outs:
            out_ref[...] = value.astype(out_ref.dtype)

    def imag(even, odd):
        value = nt_dot(even[1], odd[0]) - nt_dot(even[0], odd[1])
        for out_ref in outs:
            out_ref[...] = value.astype(out_ref.dtype)

    first, second = (imag, real) if flip else (real, imag)

    @pl.when(core_ref[0] == 0)
    def _():
        first(own_ref, other_ref)

    @pl.when(core_ref[0] != 0)
    def _():
        second(other_ref, own_ref)


def partial_kernel(rows, chain, stay, waits, passed, place_ref, mom_ref, v_ref, *refs):
    away_ref, keep_ref, *refs = refs[waits + passed :]
    left_ref, right_ref, cos_ref, sin_ref = refs[passed:]
    num_vec, sites = v_ref.shape[2], v_ref.shape[3]
    colours, momenta = v_ref.shape[1], mom_ref.shape[0]
    height = chain * rows
    zed, why, core = place_ref[0], place_ref[1], place_ref[2]
    position = (zed * PAIR + why) * CORES + core
    target_y = why if stay else 1 - why
    for part in range(2):
        for c in range(colours):
            right_ref[pl.ds(part * num_vec, num_vec), pl.ds(c * sites, sites)] = v_ref[part, c]
    site = position * sites + lax.broadcasted_iota(jnp.int32, (momenta, sites), 1)
    coord_x = site & (EXTENT - 1)
    coord_y = lax.div(site, EXTENT) & (EXTENT - 1)
    coord_z = lax.div(site, EXTENT * EXTENT)
    which = lax.broadcasted_iota(jnp.int32, (momenta, sites), 0)
    wave = jnp.zeros((momenta, sites), jnp.int32)
    for q in range(momenta):
        turned = mom_ref[q, 0] * coord_x + mom_ref[q, 1] * coord_y + mom_ref[q, 2] * coord_z
        wave = jnp.where(which == q, turned & (EXTENT - 1), wave)
    angle = wave.astype(jnp.float32) * (2.0 * math.pi / EXTENT)
    cos_ref[...] = jnp.cos(angle)
    sin_ref[...] = jnp.sin(angle)
    for keep, out_ref in ((False, away_ref), (True, keep_ref)):
        side = core if keep else 1 - core
        base = keep * 2 * height
        for turn in range(chain):
            target_z = zed ^ turn
            first = ((target_z * PAIR + target_y) * CORES + side) * rows
            momentum = lax.div(first, num_vec)
            start = pl.multiple_of(lax.rem(first, num_vec), rows)
            cosine, sine = cos_ref[pl.ds(momentum, 1), :], sin_ref[pl.ds(momentum, 1), :]
            for c in range(colours):
                vec_re = v_ref[0, c, pl.ds(start, rows), :].astype(jnp.float32)
                vec_im = v_ref[1, c, pl.ds(start, rows), :].astype(jnp.float32)
                column = pl.ds(c * sites, sites)
                left_ref[pl.ds(base + turn * rows, rows), column] = (
                    vec_re * cosine - vec_im * sine
                ).astype(jnp.bfloat16)
                left_ref[pl.ds(base + height + turn * rows, rows), column] = (
                    vec_re * sine + vec_im * cosine
                ).astype(jnp.bfloat16)
        both = nt_dot(left_ref[pl.ds(base, 2 * height), :], right_ref[...])
        out_ref[:, :num_vec] = (both[:height, :num_vec] + both[height:, num_vec:]).astype(out_ref.dtype)
        out_ref[:, num_vec:] = (both[:height, num_vec:] - both[height:, :num_vec]).astype(out_ref.dtype)


def partial_rows(rows, chain, stay, place, momenta, vectors, after=(), passed=()):
    _, colours, num_vec, sites = vectors.shape
    depth = colours * sites
    height = chain * rows
    return pl.pallas_call(
        functools.partial(partial_kernel, rows, chain, stay, len(after), len(passed)),
        out_shape=(
            jax.ShapeDtypeStruct((height, 2 * num_vec), jnp.bfloat16),
            jax.ShapeDtypeStruct((height, 2 * num_vec), jnp.float32),
        )
        + tuple(jax.ShapeDtypeStruct(block.shape, block.dtype) for block in passed),
        in_specs=[whole(pltpu.SMEM), whole(pltpu.SMEM), whole(pltpu.VMEM)]
        + [whole(pl.ANY)] * (len(after) + len(passed)),
        out_specs=(whole(pltpu.VMEM), whole(pltpu.VMEM)) + (whole(pl.ANY),) * len(passed),
        input_output_aliases={3 + len(after) + i: 2 + i for i in range(len(passed))},
        scratch_shapes=[
            pltpu.VMEM((4 * height, depth), jnp.bfloat16),
            pltpu.VMEM((2 * num_vec, depth), jnp.bfloat16),
            pltpu.VMEM((momenta.shape[0], sites), jnp.float32),
            pltpu.VMEM((momenta.shape[0], sites), jnp.float32),
        ],
        compiler_params=pltpu.CompilerParams(vmem_limit_bytes=VMEM_LIMIT),
        cost_estimate=pl.CostEstimate(flops=16 * height * depth * num_vec, bytes_accessed=vectors.size * 2 + height * num_vec * 12, transcendentals=0),
    )(place, momenta, vectors, *after, *passed)


def total_kernel(count, *refs):
    total = refs[0][...].astype(jnp.float32)
    for term in refs[1:count]:
        total = total + term[...].astype(jnp.float32)
    refs[-1][...] = total.astype(jnp.bfloat16)


def total(terms, *passed):
    def kernel(*refs):
        count = len(terms)
        total_kernel(count, *refs[:count], refs[count + len(passed)])

    return pl.pallas_call(
        kernel,
        out_shape=(jax.ShapeDtypeStruct(terms[0].shape, jnp.bfloat16),)
        + tuple(jax.ShapeDtypeStruct(block.shape, block.dtype) for block in passed),
        in_specs=[whole(pltpu.VMEM)] * len(terms) + [whole(pl.ANY)] * len(passed),
        out_specs=(whole(pltpu.VMEM),) + (whole(pl.ANY),) * len(passed),
        input_output_aliases={len(terms) + i: 1 + i for i in range(len(passed))},
        compiler_params=pltpu.CompilerParams(vmem_limit_bytes=VMEM_LIMIT),
        cost_estimate=pl.CostEstimate(flops=4 * terms[0].size, bytes_accessed=10 * terms[0].size, transcendentals=0),
    )(*terms, *passed)


def choose(flag, near, inside, outside, *after):
    count = len(inside)

    def kernel(flag_ref, near_ref, *refs):
        out_ref = refs[2 * count + len(after)]
        out_ref[0] = near_ref[...]
        for wanted, sources in ((True, refs[:count]), (False, refs[count : 2 * count])):

            @pl.when((flag_ref[0] == 1) == wanted)
            def _():
                for at, source in enumerate(sources):
                    out_ref[1 + at] = source[...]

    return pl.pallas_call(
        kernel,
        out_shape=jax.ShapeDtypeStruct((1 + count, *near.shape), near.dtype),
        in_specs=[whole(pltpu.SMEM)] + [whole(pltpu.VMEM)] * (1 + 2 * count) + [whole(pl.ANY)] * len(after),
        out_specs=whole(pltpu.VMEM),
        compiler_params=pltpu.CompilerParams(vmem_limit_bytes=VMEM_LIMIT),
        cost_estimate=pl.CostEstimate(flops=near.size, bytes_accessed=12 * near.size, transcendentals=0),
    )(flag, near, *inside, *outside, *after)


def hold(after, *passed):
    def kernel(*refs):
        pass

    return pl.pallas_call(
        kernel,
        out_shape=tuple(jax.ShapeDtypeStruct(block.shape, block.dtype) for block in passed),
        in_specs=[whole(pl.ANY)] * (len(passed) + 1),
        out_specs=(whole(pl.ANY),) * len(passed),
        input_output_aliases={i: i for i in range(len(passed))},
        compiler_params=pltpu.CompilerParams(vmem_limit_bytes=VMEM_LIMIT),
    )(*passed, after)


def owner_products(core, stacked, own, other, even_ref, odd_ref):
    rows = even_ref.shape[0]
    num_vec = own.shape[1]
    for direct, ref in ((True, even_ref), (False, odd_ref)):
        product = nn_dot if direct else nt_dot
        by_own, by_other = product(stacked, own), product(stacked, other)
        by_real = jnp.where(core == 0, by_own, by_other)
        by_imag = jnp.where(core == 0, by_other, by_own)
        if direct:
            real = by_real[:rows] - by_imag[rows:]
            imag = by_imag[:rows] + by_real[rows:]
        else:
            real = by_real[:rows] + by_imag[rows:]
            imag = by_real[rows:] - by_imag[:rows]
        ref[:, :num_vec] = real.astype(jnp.bfloat16)
        ref[:, num_vec:] = imag.astype(jnp.bfloat16)


def squares(refs):
    found = []
    for ref in refs:
        found += [ref] if len(ref.shape) == 2 else [ref.at[at] for at in range(ref.shape[0])]
    return found


def rows_kernel(arrivals, blocks, core_ref, *refs):
    terms, refs = refs[:arrivals], refs[arrivals:]
    own, other = squares(refs[:blocks]), squares(refs[blocks : 2 * blocks])
    stacked_ref, full_ref = refs[2 * blocks :]
    num_vec = terms[0].shape[1] // 2
    total = terms[0][...].astype(jnp.float32)
    for term in terms[1:]:
        total = total + term[...].astype(jnp.float32)
    elemental = total.astype(jnp.bfloat16)
    stacked = jnp.concatenate([elemental[:, :num_vec], elemental[:, num_vec:]], axis=0)
    stacked_ref[...] = stacked
    for slot, (mine, twin) in enumerate(zip(own, other)):
        even, odd = full_ref.at[2 * slot], full_ref.at[2 * slot + 1]
        owner_products(core_ref[0], stacked, mine[...], twin[...], even, odd)


def pick_kernel(blocks, group, core_ref, stacked_ref, first_ref, *refs):
    own, other = squares(refs[:blocks]), squares(refs[blocks : 2 * blocks])
    pick_ref, out_ref, last_ref = refs[2 * blocks :]
    rows, fanout, width = out_ref.shape
    stacked = stacked_ref[...]
    for slot, (mine, twin) in enumerate(zip(own, other)):
        even, odd = last_ref.at[2 * slot], last_ref.at[2 * slot + 1]
        owner_products(core_ref[0], stacked, mine[...], twin[...], even, odd)
    for block in range(rows // group):
        there = pl.ds(block * group, group)
        table = jnp.concatenate(
            [ref[:, there, :].reshape(ref.shape[0] * group, width) for ref in (first_ref, last_ref)], axis=0
        )
        picked = nn_dot(pick_ref[pl.ds(block * group * fanout, group * fanout), :], table)
        out_ref[there] = picked.astype(jnp.bfloat16).reshape(group, fanout, width)


def named(name, step):
    with jax.named_scope(name):
        return step()


def gather_plan(eigvecs, momenta, peram, graph):
    num_vec = eigvecs.shape[1]
    spaces = lax.axis_size("space")
    chain = spaces // (PAIR * CORES)
    rows = momenta.shape[0] * num_vec // spaces
    fanout = graph.shape[1]
    here = lax.axis_index("space")
    zed, why, core = here // (PAIR * CORES), here // CORES % PAIR, here % CORES
    place = jnp.stack([zed, why, core]).astype(jnp.int32)
    core_at = place[2:]

    def index(z, y, c):
        return (z * PAIR + y) * CORES + c

    def send(block, moves):
        route = [
            (index(a, y, c), index(b, y, c))
            for a, b in moves
            for y in range(PAIR)
            for c in range(CORES)
        ]
        return lax.ppermute(block, "space", route)

    def across(block):
        return lax.ppermute(block, "space", [(i, i ^ CORES) for i in range(spaces)])

    def swap(block):
        return lax.ppermute(block, "space", [(i, i ^ 1) for i in range(spaces)])

    with jax.named_scope("matrices"):
        mine = peram[0]
        theirs = named("swapP", lambda: swap(mine))

        def matrix(flip, copies, *passed):
            square = jax.ShapeDtypeStruct((num_vec, num_vec), jnp.bfloat16)
            return pl.pallas_call(
                functools.partial(product_kernel, flip, copies, len(passed)),
                out_shape=(square,) * (copies + len(passed)),
                in_specs=[whole(pltpu.SMEM)] + [whole(pltpu.VMEM)] * 2 + [whole(pl.ANY)] * len(passed),
                out_specs=(whole(pltpu.VMEM),) * copies + (whole(pl.ANY),) * len(passed),
                input_output_aliases={3 + i: copies + i for i in range(len(passed))},
                compiler_params=pltpu.CompilerParams(vmem_limit_bytes=VMEM_LIMIT),
                cost_estimate=pl.CostEstimate(
                    flops=4 * num_vec**3, bytes_accessed=10 * num_vec**2, transcendentals=0
                ),
            )(core_at, mine, theirs, *passed)

        own, lone = matrix(False, 2)
    inner = ((zed > 0) & (zed < chain - 1)).astype(jnp.int32).reshape(1)
    half = chain * rows
    with jax.named_scope("elementals"):
        vectors = jnp.transpose(eigvecs, (0, 2, 1, 3))
        away_cross, kept_cross = partial_rows(rows, chain, False, place, momenta, vectors)
        away_stay, kept_stay, lone = partial_rows(
            rows, chain, True, place, momenta, vectors, (own,), (lone,)
        )
        got_cross = named("swapA", lambda: swap(away_cross))
    with jax.named_scope("spread"):
        near = named("near", lambda: send(own, [(0, 1), (1, 0), (2, 3), (3, 2)]))
        middle = named("middle", lambda: send(own, [(1, 2), (2, 1)]))
        beside = named("beside", lambda: across(own))
    with jax.named_scope("elementals"):
        outgoing, near, middle, beside, away_stay = total(
            [kept_cross, got_cross], near, middle, beside, away_stay
        )
        crossed = named("RSy", lambda: across(outgoing))
        got_stay = named("swapB", lambda: swap(away_stay))
    with jax.named_scope("spread"):
        twin, near, middle = matrix(True, 1, near, middle)
        third_in = named("third_in", lambda: send(near, [(1, 2), (2, 1)]))
        third_out = named("third_out", lambda: send(middle, [(1, 0), (2, 3)]))
        ends = named("ends", lambda: send(lone, [(0, 3), (3, 0)]))
        twin_beside = named("swE", lambda: swap(beside))
        triple = choose(inner, near, (third_in, middle), (third_out, ends), crossed)
        twin_triple = named("swE", lambda: swap(triple))
        beside_triple = named("Y", lambda: across(triple))
        early = [own, beside, triple, twin, twin_beside, twin_triple]
    with jax.named_scope("elementals"):
        (summed,) = total([kept_stay, got_stay, crossed])
    with jax.named_scope("elementals"):
        terms = [summed[:rows]]
        for shift in range(1, chain):
            moves = [(z, z ^ shift) for z in range(chain)]
            chunk = summed[shift * rows : (shift + 1) * rows]
            terms.append(named("RSz", lambda: send(chunk, moves)))
    with jax.named_scope("pick"):
        group = 16
        near_z, third_z, fourth_z = zed ^ 1, (zed + 2) % chain, chain - 1 - zed
        chips = []
        for z, y in (
            (zed, why),
            (zed, 1 - why),
            (near_z, why),
            (third_z, why),
            (fourth_z, why),
            (near_z, 1 - why),
            (third_z, 1 - why),
            (fourth_z, 1 - why),
        ):
            chips.append(z * PAIR + y)
        columns = jnp.arange(spaces * group, dtype=jnp.int32)
        slot_of = columns // (CORES * group)
        owner_of = columns // group % CORES
        for slot, chip in enumerate(chips):
            owner_of = owner_of + jnp.where(slot_of == slot, chip * CORES, 0)
        row_of = jnp.arange(rows * fanout, dtype=jnp.int32) // fanout % group
        pick = (
            (graph.reshape(-1)[:, None] == owner_of[None, :])
            & (row_of[:, None] == (columns % group)[None, :])
        ).astype(jnp.bfloat16)
    with jax.named_scope("contract"):
        slots = 1 + chain
        stacked, first = pl.pallas_call(
            functools.partial(rows_kernel, len(terms), len(early) // 2),
            out_shape=(
                jax.ShapeDtypeStruct((2 * rows, num_vec), jnp.bfloat16),
                jax.ShapeDtypeStruct((2 * slots, rows, 2 * num_vec), jnp.bfloat16),
            ),
            in_specs=[whole(pltpu.SMEM)] + [whole(pltpu.VMEM)] * (len(terms) + len(early)),
            out_specs=(whole(pltpu.VMEM), whole(pltpu.VMEM)),
            compiler_params=pltpu.CompilerParams(vmem_limit_bytes=VMEM_LIMIT),
            cost_estimate=pl.CostEstimate(
                flops=16 * slots * rows * num_vec**2,
                bytes_accessed=8 * slots * num_vec**2,
                transcendentals=0,
            ),
        )(core_at, *terms, *early)
        (beside_triple,) = hold(first, beside_triple)
        late = [beside_triple, named("swL", lambda: swap(beside_triple))]
        slots = chain - 1
        return pl.pallas_call(
            functools.partial(pick_kernel, len(late) // 2, group),
            out_shape=jax.ShapeDtypeStruct((rows, fanout, 2 * num_vec), jnp.bfloat16),
            in_specs=[whole(pltpu.SMEM)] + [whole(pltpu.VMEM)] * (2 + len(late) + 1),
            out_specs=whole(pltpu.VMEM),
            scratch_shapes=[pltpu.VMEM((2 * slots, rows, 2 * num_vec), jnp.bfloat16)],
            compiler_params=pltpu.CompilerParams(vmem_limit_bytes=VMEM_LIMIT),
            cost_estimate=pl.CostEstimate(
                flops=16 * slots * rows * num_vec**2,
                bytes_accessed=8 * slots * num_vec**2,
                transcendentals=0,
            ),
        )(core_at, stacked, first, *late, pick)


LINE = 4


def on_device(eigvecs, momenta, peram, graph):
    num_vec = eigvecs.shape[1]
    spaces = lax.axis_size("space")
    rows = momenta.shape[0] * num_vec // spaces
    if spaces == CORES * PAIR * LINE and num_vec % rows == 0 and rows % 16 == 0:
        return gather_plan(eigvecs, momenta, peram, graph)
    return exchange_plan(eigvecs, momenta, peram, graph)


def solution(mesh):
    placed = (
        P(None, None, None, ("groups", "space")),
        P(),
        P(("groups", "space"), None, None, None),
        P(("groups", "space"), None),
    )
    return jax.shard_map(
        on_device,
        mesh=mesh,
        in_specs=placed,
        out_specs=P(("groups", "space"), None, None),
        check_vma=False,
    )
```

```python
import functools
import math

import jax
import jax.numpy as jnp
from jax import lax
from jax.experimental import pallas as pl
from jax.experimental.pallas import tpu as pltpu
from jax.sharding import PartitionSpec as P

EXTENT = 128


def partner(block, axis, bit):
    count = lax.axis_size(axis)
    route = []
    for low in range(count):
        high = low | 1 << bit
        if high != low and high < count:
            route += [(low, high), (high, low)]
    return lax.ppermute(block, axis, route)


def phase_tables(momenta, site_index, extent):
    coord_x = site_index % extent
    coord_y = site_index // extent % extent
    coord_z = site_index // (extent * extent)
    wave_number = (
        momenta[:, 0:1] * coord_x[None, :]
        + momenta[:, 1:2] * coord_y[None, :]
        + momenta[:, 2:3] * coord_z[None, :]
    )
    wave_number = jnp.mod(wave_number, extent)
    phase_angle = wave_number.astype(jnp.float32) * (2.0 * math.pi / extent)
    return (jnp.cos(phase_angle), jnp.sin(phase_angle))


def block_form(peram_pair):
    peram_re = peram_pair[0]
    peram_im = peram_pair[1]
    top_half = jnp.concatenate([peram_re, peram_im], axis=1)
    bottom_half = jnp.concatenate([-peram_im, peram_re], axis=1)
    return jnp.concatenate([top_half, bottom_half], axis=0)


def sink_product(arrived, block):
    return lax.dot_general(
        arrived, block, (((2,), (0,)), ((), ())), preferred_element_type=jnp.float32
    ).astype(jnp.bfloat16)


def adjoint_product(sinks, block):
    return lax.dot_general(
        sinks, block, (((2,), (1,)), ((), ())), preferred_element_type=jnp.float32
    ).astype(jnp.bfloat16)


def exchange_plan(eigvecs, momenta, peram, graph):
    num_vec = eigvecs.shape[1]
    local_sites = eigvecs.shape[3]
    spaces = lax.axis_size("space")
    position = lax.axis_index("space")
    site_index = position * local_sites + jnp.arange(local_sites, dtype=jnp.int32)
    cosine, sine = phase_tables(momenta, site_index, EXTENT)
    total_rows = cosine.shape[0] * num_vec
    rows_here = total_rows // spaces
    right_side = jnp.concatenate(
        [
            jnp.concatenate([eigvecs[0], -eigvecs[1]], axis=1),
            jnp.concatenate([eigvecs[1], eigvecs[0]], axis=1),
        ],
        axis=0,
    ).reshape(2 * num_vec, 6 * local_sites)
    row_index = jnp.arange(rows_here * lax.axis_size("space"), dtype=jnp.int32)
    vector_index = row_index % num_vec
    momentum_index = row_index // num_vec
    vec_re = jnp.take(eigvecs[0], vector_index, axis=0).astype(jnp.float32)
    vec_im = jnp.take(eigvecs[1], vector_index, axis=0).astype(jnp.float32)
    cos_rows = jnp.take(cosine, momentum_index, axis=0)[:, None, :]
    sin_rows = jnp.take(sine, momentum_index, axis=0)[:, None, :]
    left_re = vec_re * cos_rows - vec_im * sin_rows
    left_im = -(vec_re * sin_rows + vec_im * cos_rows)
    left_cat = (
        jnp.concatenate([left_re, left_im], axis=1)
        .astype(jnp.bfloat16)
        .reshape(rows_here * lax.axis_size("space"), 6 * local_sites)
    )
    summed = lax.psum_scatter(
        lax.dot_general(
            left_cat, right_side, (((1,), (1,)), ((), ())), preferred_element_type=jnp.float32
        ),
        "space",
        scatter_dimension=0,
        tiled=True,
    )
    elemental = summed.astype(jnp.bfloat16)
    fanout = graph.shape[1]
    capacity = max(2, 2 * rows_here * fanout // spaces)
    flat_owner = graph.reshape(-1)
    entries = flat_owner.shape[0]
    onehot = (flat_owner[:, None] == jnp.arange(spaces, dtype=jnp.int32)[None, :]).astype(jnp.int32)
    earlier = jnp.cumsum(onehot, axis=0) - onehot
    slot = jnp.sum(earlier * onehot, axis=1)
    source_row = jnp.arange(entries, dtype=jnp.int32) // fanout
    payload = jnp.take(elemental, source_row, axis=0)
    outgoing = (
        jnp.zeros((spaces, capacity, 2 * num_vec), jnp.bfloat16).at[flat_owner, slot].set(payload)
    )
    own_block = block_form(peram[0])
    partner_block = partner(own_block, "space", 0)
    sinks = sink_product(
        lax.all_to_all(outgoing, "space", split_axis=0, concat_axis=0, tiled=True), own_block
    )
    finished = adjoint_product(sinks, partner_block)
    returned = lax.all_to_all(finished, "space", split_axis=0, concat_axis=0, tiled=True)
    collected = returned[flat_owner, slot]
    return collected.reshape(rows_here, fanout, 2 * num_vec)


CORES = 2
PAIR = 2
VMEM_LIMIT = 20 * 1024 * 1024


def whole(space):
    return pl.BlockSpec(memory_space=space)


def nt_dot(left, right):
    return lax.dot_general(
        left, right, (((1,), (1,)), ((), ())), preferred_element_type=jnp.float32
    )


def nn_dot(left, right):
    return lax.dot_general(
        left, right, (((1,), (0,)), ((), ())), preferred_element_type=jnp.float32
    )


def product_kernel(flip, copies, waits, core_ref, own_ref, other_ref, *refs):
    outs = refs[waits : waits + copies]

    def real(even, odd):
        value = nt_dot(even[0], odd[0]) + nt_dot(even[1], odd[1])
        for out_ref in outs:
            out_ref[...] = value.astype(out_ref.dtype)

    def imag(even, odd):
        value = nt_dot(even[1], odd[0]) - nt_dot(even[0], odd[1])
        for out_ref in outs:
            out_ref[...] = value.astype(out_ref.dtype)

    first, second = (imag, real) if flip else (real, imag)

    @pl.when(core_ref[0] == 0)
    def _():
        first(own_ref, other_ref)

    @pl.when(core_ref[0] != 0)
    def _():
        second(other_ref, own_ref)


def partial_kernel(rows, chain, stay, waits, passed, place_ref, mom_ref, v_ref, *refs):
    away_ref, keep_ref, *refs = refs[waits + passed :]
    left_ref, right_ref, cos_ref, sin_ref = refs[passed:]
    num_vec, sites = v_ref.shape[2], v_ref.shape[3]
    colours, momenta = v_ref.shape[1], mom_ref.shape[0]
    height = chain * rows
    zed, why, core = place_ref[0], place_ref[1], place_ref[2]
    position = (zed * PAIR + why) * CORES + core
    target_y = why if stay else 1 - why
    for part in range(2):
        for c in range(colours):
            right_ref[pl.ds(part * num_vec, num_vec), pl.ds(c * sites, sites)] = v_ref[part, c]
    site = position * sites + lax.broadcasted_iota(jnp.int32, (momenta, sites), 1)
    coord_x = site & (EXTENT - 1)
    coord_y = lax.div(site, EXTENT) & (EXTENT - 1)
    coord_z = lax.div(site, EXTENT * EXTENT)
    which = lax.broadcasted_iota(jnp.int32, (momenta, sites), 0)
    wave = jnp.zeros((momenta, sites), jnp.int32)
    for q in range(momenta):
        turned = mom_ref[q, 0] * coord_x + mom_ref[q, 1] * coord_y + mom_ref[q, 2] * coord_z
        wave = jnp.where(which == q, turned & (EXTENT - 1), wave)
    angle = wave.astype(jnp.float32) * (2.0 * math.pi / EXTENT)
    cos_ref[...] = jnp.cos(angle)
    sin_ref[...] = jnp.sin(angle)
    for keep, out_ref in ((False, away_ref), (True, keep_ref)):
        side = core if keep else 1 - core
        base = keep * 2 * height
        for turn in range(chain):
            target_z = zed ^ turn
            first = ((target_z * PAIR + target_y) * CORES + side) * rows
            momentum = lax.div(first, num_vec)
            start = pl.multiple_of(lax.rem(first, num_vec), rows)
            cosine, sine = cos_ref[pl.ds(momentum, 1), :], sin_ref[pl.ds(momentum, 1), :]
            for c in range(colours):
                vec_re = v_ref[0, c, pl.ds(start, rows), :].astype(jnp.float32)
                vec_im = v_ref[1, c, pl.ds(start, rows), :].astype(jnp.float32)
                column = pl.ds(c * sites, sites)
                left_ref[pl.ds(base + turn * rows, rows), column] = (
                    vec_re * cosine - vec_im * sine
                ).astype(jnp.bfloat16)
                left_ref[pl.ds(base + height + turn * rows, rows), column] = (
                    vec_re * sine + vec_im * cosine
                ).astype(jnp.bfloat16)
        both = nt_dot(left_ref[pl.ds(base, 2 * height), :], right_ref[...])
        out_ref[:, :num_vec] = (both[:height, :num_vec] + both[height:, num_vec:]).astype(out_ref.dtype)
        out_ref[:, num_vec:] = (both[:height, num_vec:] - both[height:, :num_vec]).astype(out_ref.dtype)


def partial_rows(rows, chain, stay, place, momenta, vectors, after=(), passed=()):
    _, colours, num_vec, sites = vectors.shape
    depth = colours * sites
    height = chain * rows
    return pl.pallas_call(
        functools.partial(partial_kernel, rows, chain, stay, len(after), len(passed)),
        out_shape=(
            jax.ShapeDtypeStruct((height, 2 * num_vec), jnp.bfloat16),
            jax.ShapeDtypeStruct((height, 2 * num_vec), jnp.float32),
        )
        + tuple(jax.ShapeDtypeStruct(block.shape, block.dtype) for block in passed),
        in_specs=[whole(pltpu.SMEM), whole(pltpu.SMEM), whole(pltpu.VMEM)]
        + [whole(pl.ANY)] * (len(after) + len(passed)),
        out_specs=(whole(pltpu.VMEM), whole(pltpu.VMEM)) + (whole(pl.ANY),) * len(passed),
        input_output_aliases={3 + len(after) + i: 2 + i for i in range(len(passed))},
        scratch_shapes=[
            pltpu.VMEM((4 * height, depth), jnp.bfloat16),
            pltpu.VMEM((2 * num_vec, depth), jnp.bfloat16),
            pltpu.VMEM((momenta.shape[0], sites), jnp.float32),
            pltpu.VMEM((momenta.shape[0], sites), jnp.float32),
        ],
        compiler_params=pltpu.CompilerParams(vmem_limit_bytes=VMEM_LIMIT),
        cost_estimate=pl.CostEstimate(flops=16 * height * depth * num_vec, bytes_accessed=vectors.size * 2 + height * num_vec * 12, transcendentals=0),
    )(place, momenta, vectors, *after, *passed)


def total_kernel(count, *refs):
    total = refs[0][...].astype(jnp.float32)
    for term in refs[1:count]:
        total = total + term[...].astype(jnp.float32)
    refs[-1][...] = total.astype(jnp.bfloat16)


def total(terms, *passed):
    def kernel(*refs):
        count = len(terms)
        total_kernel(count, *refs[:count], refs[count + len(passed)])

    return pl.pallas_call(
        kernel,
        out_shape=(jax.ShapeDtypeStruct(terms[0].shape, jnp.bfloat16),)
        + tuple(jax.ShapeDtypeStruct(block.shape, block.dtype) for block in passed),
        in_specs=[whole(pltpu.VMEM)] * len(terms) + [whole(pl.ANY)] * len(passed),
        out_specs=(whole(pltpu.VMEM),) + (whole(pl.ANY),) * len(passed),
        input_output_aliases={len(terms) + i: 1 + i for i in range(len(passed))},
        compiler_params=pltpu.CompilerParams(vmem_limit_bytes=VMEM_LIMIT),
        cost_estimate=pl.CostEstimate(flops=4 * terms[0].size, bytes_accessed=10 * terms[0].size, transcendentals=0),
    )(*terms, *passed)


def choose(flag, near, inside, outside, *after):
    count = len(inside)

    def kernel(flag_ref, near_ref, *refs):
        out_ref = refs[2 * count + len(after)]
        out_ref[0] = near_ref[...]
        for wanted, sources in ((True, refs[:count]), (False, refs[count : 2 * count])):

            @pl.when((flag_ref[0] == 1) == wanted)
            def _():
                for at, source in enumerate(sources):
                    out_ref[1 + at] = source[...]

    return pl.pallas_call(
        kernel,
        out_shape=jax.ShapeDtypeStruct((1 + count, *near.shape), near.dtype),
        in_specs=[whole(pltpu.SMEM)] + [whole(pltpu.VMEM)] * (1 + 2 * count) + [whole(pl.ANY)] * len(after),
        out_specs=whole(pltpu.VMEM),
        compiler_params=pltpu.CompilerParams(vmem_limit_bytes=VMEM_LIMIT),
        cost_estimate=pl.CostEstimate(flops=near.size, bytes_accessed=12 * near.size, transcendentals=0),
    )(flag, near, *inside, *outside, *after)


def hold(after, *passed):
    def kernel(*refs):
        pass

    return pl.pallas_call(
        kernel,
        out_shape=tuple(jax.ShapeDtypeStruct(block.shape, block.dtype) for block in passed),
        in_specs=[whole(pl.ANY)] * (len(passed) + 1),
        out_specs=(whole(pl.ANY),) * len(passed),
        input_output_aliases={i: i for i in range(len(passed))},
        compiler_params=pltpu.CompilerParams(vmem_limit_bytes=VMEM_LIMIT),
    )(*passed, after)


def owner_products(core, stacked, own, other, even_ref, odd_ref):
    rows = even_ref.shape[0]
    num_vec = own.shape[1]
    for direct, ref in ((True, even_ref), (False, odd_ref)):
        product = nn_dot if direct else nt_dot
        by_own, by_other = product(stacked, own), product(stacked, other)
        by_real = jnp.where(core == 0, by_own, by_other)
        by_imag = jnp.where(core == 0, by_other, by_own)
        if direct:
            real = by_real[:rows] - by_imag[rows:]
            imag = by_imag[:rows] + by_real[rows:]
        else:
            real = by_real[:rows] + by_imag[rows:]
            imag = by_real[rows:] - by_imag[:rows]
        ref[:, :num_vec] = real.astype(jnp.bfloat16)
        ref[:, num_vec:] = imag.astype(jnp.bfloat16)


def squares(refs):
    found = []
    for ref in refs:
        found += [ref] if len(ref.shape) == 2 else [ref.at[at] for at in range(ref.shape[0])]
    return found


def rows_kernel(arrivals, blocks, core_ref, *refs):
    terms, refs = refs[:arrivals], refs[arrivals:]
    own, other = squares(refs[:blocks]), squares(refs[blocks : 2 * blocks])
    stacked_ref, full_ref = refs[2 * blocks :]
    num_vec = terms[0].shape[1] // 2
    total = terms[0][...].astype(jnp.float32)
    for term in terms[1:]:
        total = total + term[...].astype(jnp.float32)
    elemental = total.astype(jnp.bfloat16)
    stacked = jnp.concatenate([elemental[:, :num_vec], elemental[:, num_vec:]], axis=0)
    stacked_ref[...] = stacked
    for slot, (mine, twin) in enumerate(zip(own, other)):
        even, odd = full_ref.at[2 * slot], full_ref.at[2 * slot + 1]
        owner_products(core_ref[0], stacked, mine[...], twin[...], even, odd)


def pick_kernel(blocks, group, core_ref, stacked_ref, first_ref, *refs):
    own, other = squares(refs[:blocks]), squares(refs[blocks : 2 * blocks])
    pick_ref, out_ref, last_ref = refs[2 * blocks :]
    rows, fanout, width = out_ref.shape
    stacked = stacked_ref[...]
    for slot, (mine, twin) in enumerate(zip(own, other)):
        even, odd = last_ref.at[2 * slot], last_ref.at[2 * slot + 1]
        owner_products(core_ref[0], stacked, mine[...], twin[...], even, odd)
    for block in range(rows // group):
        there = pl.ds(block * group, group)
        table = jnp.concatenate(
            [ref[:, there, :].reshape(ref.shape[0] * group, width) for ref in (first_ref, last_ref)], axis=0
        )
        picked = nn_dot(pick_ref[pl.ds(block * group * fanout, group * fanout), :], table)
        out_ref[there] = picked.astype(jnp.bfloat16).reshape(group, fanout, width)


def named(name, step):
    with jax.named_scope(name):
        return step()


def gather_plan(eigvecs, momenta, peram, graph):
    num_vec = eigvecs.shape[1]
    spaces = lax.axis_size("space")
    chain = spaces // (PAIR * CORES)
    rows = momenta.shape[0] * num_vec // spaces
    fanout = graph.shape[1]
    here = lax.axis_index("space")
    zed, why, core = here // (PAIR * CORES), here // CORES % PAIR, here % CORES
    place = jnp.stack([zed, why, core]).astype(jnp.int32)
    core_at = place[2:]

    def index(z, y, c):
        return (z * PAIR + y) * CORES + c

    def send(block, moves):
        route = [
            (index(a, y, c), index(b, y, c))
            for a, b in moves
            for y in range(PAIR)
            for c in range(CORES)
        ]
        return lax.ppermute(block, "space", route)

    def across(block):
        return lax.ppermute(block, "space", [(i, i ^ CORES) for i in range(spaces)])

    def swap(block):
        return lax.ppermute(block, "space", [(i, i ^ 1) for i in range(spaces)])

    with jax.named_scope("matrices"):
        mine = peram[0]
        theirs = named("swapP", lambda: swap(mine))

        def matrix(flip, copies, *passed):
            square = jax.ShapeDtypeStruct((num_vec, num_vec), jnp.bfloat16)
            return pl.pallas_call(
                functools.partial(product_kernel, flip, copies, len(passed)),
                out_shape=(square,) * (copies + len(passed)),
                in_specs=[whole(pltpu.SMEM)] + [whole(pltpu.VMEM)] * 2 + [whole(pl.ANY)] * len(passed),
                out_specs=(whole(pltpu.VMEM),) * copies + (whole(pl.ANY),) * len(passed),
                input_output_aliases={3 + i: copies + i for i in range(len(passed))},
                compiler_params=pltpu.CompilerParams(vmem_limit_bytes=VMEM_LIMIT),
                cost_estimate=pl.CostEstimate(
                    flops=4 * num_vec**3, bytes_accessed=10 * num_vec**2, transcendentals=0
                ),
            )(core_at, mine, theirs, *passed)

        own, lone = matrix(False, 2)
    inner = ((zed > 0) & (zed < chain - 1)).astype(jnp.int32).reshape(1)
    half = chain * rows
    with jax.named_scope("elementals"):
        vectors = jnp.transpose(eigvecs, (0, 2, 1, 3))
        away_cross, kept_cross = partial_rows(rows, chain, False, place, momenta, vectors)
        away_stay, kept_stay, lone = partial_rows(
            rows, chain, True, place, momenta, vectors, (own,), (lone,)
        )
        got_cross = named("swapA", lambda: swap(away_cross))
    with jax.named_scope("spread"):
        near = named("near", lambda: send(own, [(0, 1), (1, 0), (2, 3), (3, 2)]))
        middle = named("middle", lambda: send(own, [(1, 2), (2, 1)]))
        beside = named("beside", lambda: across(own))
    with jax.named_scope("elementals"):
        outgoing, near, middle, away_stay = total([kept_cross, got_cross], near, middle, away_stay)
        crossed = named("RSy", lambda: across(outgoing))
        got_stay = named("swapB", lambda: swap(away_stay))
    with jax.named_scope("spread"):
        twin, near, middle, beside = matrix(True, 1, near, middle, beside)
        third_in = named("third_in", lambda: send(near, [(1, 2), (2, 1)]))
        third_out = named("third_out", lambda: send(middle, [(1, 0), (2, 3)]))
        ends = named("ends", lambda: send(lone, [(0, 3), (3, 0)]))
        twin_beside = named("swE", lambda: swap(beside))
        triple = choose(inner, near, (third_in, middle), (third_out, ends), crossed)
        twin_triple = named("swE", lambda: swap(triple))
        beside_triple = named("Y", lambda: across(triple))
        early = [own, beside, triple, twin, twin_beside, twin_triple]
    with jax.named_scope("elementals"):
        (summed,) = total([kept_stay, got_stay, crossed])
    with jax.named_scope("elementals"):
        terms = [summed[:rows]]
        for shift in range(1, chain):
            moves = [(z, z ^ shift) for z in range(chain)]
            chunk = summed[shift * rows : (shift + 1) * rows]
            terms.append(named("RSz", lambda: send(chunk, moves)))
    with jax.named_scope("pick"):
        group = 16
        near_z, third_z, fourth_z = zed ^ 1, (zed + 2) % chain, chain - 1 - zed
        chips = []
        for z, y in (
            (zed, why),
            (zed, 1 - why),
            (near_z, why),
            (third_z, why),
            (fourth_z, why),
            (near_z, 1 - why),
            (third_z, 1 - why),
            (fourth_z, 1 - why),
        ):
            chips.append(z * PAIR + y)
        columns = jnp.arange(spaces * group, dtype=jnp.int32)
        slot_of = columns // (CORES * group)
        owner_of = columns // group % CORES
        for slot, chip in enumerate(chips):
            owner_of = owner_of + jnp.where(slot_of == slot, chip * CORES, 0)
        row_of = jnp.arange(rows * fanout, dtype=jnp.int32) // fanout % group
        pick = (
            (graph.reshape(-1)[:, None] == owner_of[None, :])
            & (row_of[:, None] == (columns % group)[None, :])
        ).astype(jnp.bfloat16)
    with jax.named_scope("contract"):
        slots = 1 + chain
        stacked, first = pl.pallas_call(
            functools.partial(rows_kernel, len(terms), len(early) // 2),
            out_shape=(
                jax.ShapeDtypeStruct((2 * rows, num_vec), jnp.bfloat16),
                jax.ShapeDtypeStruct((2 * slots, rows, 2 * num_vec), jnp.bfloat16),
            ),
            in_specs=[whole(pltpu.SMEM)] + [whole(pltpu.VMEM)] * (len(terms) + len(early)),
            out_specs=(whole(pltpu.VMEM), whole(pltpu.VMEM)),
            compiler_params=pltpu.CompilerParams(vmem_limit_bytes=VMEM_LIMIT),
            cost_estimate=pl.CostEstimate(
                flops=16 * slots * rows * num_vec**2,
                bytes_accessed=8 * slots * num_vec**2,
                transcendentals=0,
            ),
        )(core_at, *terms, *early)
        (beside_triple,) = hold(first, beside_triple)
        late = [beside_triple, named("swL", lambda: swap(beside_triple))]
        slots = chain - 1
        return pl.pallas_call(
            functools.partial(pick_kernel, len(late) // 2, group),
            out_shape=jax.ShapeDtypeStruct((rows, fanout, 2 * num_vec), jnp.bfloat16),
            in_specs=[whole(pltpu.SMEM)] + [whole(pltpu.VMEM)] * (2 + len(late) + 1),
            out_specs=whole(pltpu.VMEM),
            scratch_shapes=[pltpu.VMEM((2 * slots, rows, 2 * num_vec), jnp.bfloat16)],
            compiler_params=pltpu.CompilerParams(vmem_limit_bytes=VMEM_LIMIT),
            cost_estimate=pl.CostEstimate(
                flops=16 * slots * rows * num_vec**2,
                bytes_accessed=8 * slots * num_vec**2,
                transcendentals=0,
            ),
        )(core_at, stacked, first, *late, pick)


LINE = 4


def on_device(eigvecs, momenta, peram, graph):
    num_vec = eigvecs.shape[1]
    spaces = lax.axis_size("space")
    rows = momenta.shape[0] * num_vec // spaces
    if spaces == CORES * PAIR * LINE and num_vec % rows == 0 and rows % 16 == 0:
        return gather_plan(eigvecs, momenta, peram, graph)
    return exchange_plan(eigvecs, momenta, peram, graph)


def solution(mesh):
    placed = (
        P(None, None, None, ("groups", "space")),
        P(),
        P(("groups", "space"), None, None, None),
        P(("groups", "space"), None),
    )
    return jax.shard_map(
        on_device,
        mesh=mesh,
        in_specs=placed,
        out_specs=P(("groups", "space"), None, None),
        check_vma=False,
    )
```
